1024 devices in a mesh: gx: 16 (over y, core), gy: 16 (over z_hi, x), gz: 4 (over z_lo).
Axes of the slice: x: 4, y: 8, z: 16 (z_hi: 4, z_lo: 4; z = z_hi * 4 + z_lo), core: 2. Of those that a mesh axis runs over, the one named last changes fastest.
Arguments:
- positions: float32 [3, 16, 16, 4, 192], P(None, 'gx', 'gy', 'gz'), may hold values from 0 to 8, as said below
- polarizability: float32 [16, 16, 4, 192], P('gx', 'gy', 'gz'), may hold values from 0.01 to 0.06
- direct_field: float32 [3, 16, 16, 4, 192], P(None, 'gx', 'gy', 'gz'), may hold values from -150 to 150
- groups: int32 [16, 16, 4, 192], P('gx', 'gy', 'gz'), may hold values from 0 to 47, never falling along the last dimension, each value on 1 to 8 neighbouring positions
Outputs:
- dipoles: float32 [3, 16, 16, 4, 192], P(None, 'gx', 'gy', 'gz')
- gradient: float32 [3, 16, 16, 4, 192], P(None, 'gx', 'gy', 'gz')
- energy: float32 [], replicated
The draws below stay inside these ranges and needn't reach their ends.
Inputs may be any that keep to these rules, and one draw needn't show every extreme that they name: `positions`: atoms of a domain sit one to a lattice site of 8 x 8 x 3 sites of spacing 1, in the order x, y, normal (the normal fastest), each within 0.2 of its site along every component, so no two atoms are closer than 0.6. `groups`: along the atoms of one domain the ids never fall; each group holds 1 to 8 atoms.
All inputs are finite; a program needn't handle non-finite values.
Results may differ from the reference program's by a relative error of at most 0.0003.
Values sent between devices are 32-bit elements; how exact they have to be, the bound alone decides.
No kernel may reach another device: no remote copies, remote signals or barrier semaphores. Data moves between devices by JAX's collectives and lax.ppermute only.
A program may use at most 32 MiB of HBM per device.

```python
import math
import jax
import jax.numpy as jnp
import numpy as np
from jax import lax

LX = 8
LY = 8
DEPTH = 3
CUTOFF = 3
ATOMS_DEV = 192
ATOMS = 196608
N_GX = 16
N_GY = 16
N_GZ = 4
DEVICES = 1024


def draw_positions(key, part):
    atom_count = LX * LY * DEPTH
    site_ids = jnp.arange(atom_count, dtype=jnp.int32)
    lattice = jnp.stack([site_ids // (LY * DEPTH), site_ids // DEPTH % LY, site_ids % DEPTH]).astype(jnp.float32) + 0.5
    reach = 0.15
    jitter = jax.random.uniform(key, (3, N_GX, N_GY, N_GZ, atom_count), minval=-reach, maxval=reach)
    return lattice[:, None, None, None, :] + jitter


def draw_direct_field(key, part):
    atom_count = LX * LY * DEPTH
    domain_ids = jnp.arange(DEVICES, dtype=jnp.int32).reshape(N_GX, N_GY, N_GZ).astype(jnp.float32)
    ramp_up = domain_ids / (DEVICES - 1)
    spread = (12.0 * (1.0 + 2.0 * ramp_up))[None, :, :, :, None]
    full_shape = (3, N_GX, N_GY, N_GZ, atom_count)
    values = jnp.clip(jax.random.normal(key, full_shape), -4.0, 4.0) * spread
    return values


def block_levels(key, shape, shards, least, largest):
    def one(axis_at, shards_of):
        draws = jax.random.uniform(jax.random.fold_in(jax.random.fold_in(key, 6), axis_at), (shards_of,), jnp.float32, least / len(shards), largest / len(shards))
        return jnp.repeat(jnp.exp(draws), shape[axis_at] // shards_of).reshape((-1,) + (1,) * (len(shape) - axis_at - 1))

    gain = one(*shards[0])
    for cut in shards[1:]:
        gain = gain * one(*cut)
    return gain


def split_up(count, total, most, slope):
    portions = [(1 << 20) // math.isqrt(grade ** slope) + 1 for grade in range(2, count + 1)]
    spare, holding = total - most - (count - 1), [1] * (count - 1)
    while spare > 0:
        free = [i for i in range(count - 1) if holding[i] < most]
        pool, budget = sum([portions[i] for i in free]), spare
        for i in free:
            addition = min(most - holding[i], max(1, budget * portions[i] // pool), spare)
            holding[i] = holding[i] + addition
            spare = spare - addition
    return np.array([most] + holding)


def uneven(own_key, count, total, most, lean):
    if count == 2:
        one = jax.random.randint(own_key, (), max(1, total - most), min(most, total - 1) + 1)
        return jnp.stack([one, total - one])
    sizes = jnp.asarray(split_up(count, total, most, lean), jnp.int32)
    twos = (count - 1) // 2
    donor, sink = sizes[1:1 + 2 * twos:2], sizes[2:2 + 2 * twos:2]
    margin = jnp.minimum(donor - 1, most - sink)
    passed = jax.random.randint(jax.random.fold_in(own_key, 1), (twos,), 0, 1 << 20) % (margin + 1)
    sizes = sizes.at[1:1 + 2 * twos:2].set(donor - passed).at[2:2 + 2 * twos:2].set(sink + passed)
    return sizes[jax.random.permutation(jax.random.fold_in(own_key, 2), count)]


def setup_inputs(seed: int = 0) -> dict:
    key_of = jax.random.split(jax.random.key(seed), 5)
    return {
        "positions": draw_positions(jax.random.fold_in(key_of[4], 71), 0),
        "polarizability": jnp.clip(jnp.exp(math.log(0.06) - 1.7917595 * jax.random.uniform(key_of[1], (N_GX, N_GY, N_GZ, ATOMS_DEV), jnp.float32) ** block_levels(key_of[1], (N_GX, N_GY, N_GZ, ATOMS_DEV), ((0, 16), (1, 16), (2, 4)), -0.2, 0.2)), 0.01, 0.06),
        "direct_field": draw_direct_field(jax.random.fold_in(key_of[4], 71), 0),
        "groups": jax.vmap(lambda own: jnp.searchsorted(jnp.cumsum(uneven(own, ATOMS_DEV // 4, ATOMS_DEV, 8, 1)), jnp.arange(ATOMS_DEV), side="right"))(jax.random.split(key_of[3], N_GX * N_GY * N_GZ)).reshape((N_GX, N_GY, N_GZ, ATOMS_DEV)).astype(jnp.int32),
    }


thole_factor = 0.39
group_scale = 0.5

def tensor_parts(own_pos, own_polar, own_group, far_pos, far_polar, centre):
    atom_count = own_pos.shape[1]
    displace = far_pos[:, None, :] - own_pos[:, :, None]
    dist_sq = lax.optimization_barrier(jnp.sum(displace * displace, axis=0))
    same_atom = jnp.logical_and(centre, jnp.eye(atom_count, dtype=bool))
    same_group = jnp.logical_and(centre, own_group[:, None] == own_group[None, :])
    safe_sq = jnp.where(same_atom, 1.0, dist_sq)
    inverse = lax.rsqrt(safe_sq)
    cut_ratio = safe_sq / (CUTOFF * CUTOFF)
    smooth_cut = jnp.where(cut_ratio < 1.0, jnp.square(1.0 - cut_ratio), 0.0)
    damping = thole_factor * safe_sq * safe_sq * inverse / jnp.sqrt(own_polar[:, None] * far_polar[None, :])
    decayed = jnp.exp(-damping)
    damp_three = -jnp.expm1(-damping)
    damp_five = damp_three - damping * decayed
    weight = smooth_cut * jnp.where(same_group, group_scale, 1.0) * jnp.where(same_atom, 0.0, 1.0)
    inv_cube = inverse * inverse * inverse
    coupling3 = weight * damp_three * inv_cube
    coupling5 = 3.0 * weight * damp_five * inv_cube * inverse * inverse
    return (displace, coupling3, coupling5)

def apply_tensor(own_pos, own_polar, own_group, far_pos, far_polar, far_vector, centre_flags):
    atom_count = own_pos.shape[1]

    def advance(running, slot_item):
        pos_slot, polar_slot, vector_slot, centre = slot_item
        displace, coupling3, coupling5 = tensor_parts(own_pos, own_polar, own_group, pos_slot, polar_slot, centre)
        along = lax.optimization_barrier(jnp.sum(displace * vector_slot[:, None, :], axis=0))
        contrib = lax.optimization_barrier(jnp.sum(coupling5[None] * displace * along[None] - coupling3[None] * vector_slot[:, None, :], axis=2))
        return (running + contrib, None)
    result, _ = lax.scan(advance, jnp.zeros((3, atom_count), jnp.float32), (far_pos, far_polar, far_vector, centre_flags))
    return result

def pair_gradient(own_pos, own_polar, own_group, far_pos, far_polar, own_dip, own_adj, far_dip, far_adj, centre_flags):

    def slot_value(position, pos_slot, polar_slot, dip_slot, adj_slot, centre):
        displace, coupling3, coupling5 = tensor_parts(position, own_polar, own_group, pos_slot, polar_slot, centre)
        own_dip_along = lax.optimization_barrier(jnp.sum(displace * own_dip[:, :, None], axis=0))
        own_adj_along = lax.optimization_barrier(jnp.sum(displace * own_adj[:, :, None], axis=0))
        far_dip_along = lax.optimization_barrier(jnp.sum(displace * dip_slot[:, None, :], axis=0))
        far_adj_along = lax.optimization_barrier(jnp.sum(displace * adj_slot[:, None, :], axis=0))
        cross_terms = lax.optimization_barrier(jnp.sum(own_dip[:, :, None] * adj_slot[:, None, :] + own_adj[:, :, None] * dip_slot[:, None, :], axis=0))
        return 0.5 * jnp.sum(coupling5 * (own_dip_along * far_adj_along + own_adj_along * far_dip_along) - coupling3 * cross_terms)

    def advance(running, slot_item):
        pos_slot, polar_slot, dip_slot, adj_slot, centre = slot_item
        return (running + jax.grad(slot_value)(own_pos, pos_slot, polar_slot, dip_slot, adj_slot, centre), None)
    result, _ = lax.scan(advance, jnp.zeros(own_pos.shape, jnp.float32), (far_pos, far_polar, far_dip, far_adj, centre_flags))
    return result

def slot_table():
    slot_ids = jnp.arange(27, dtype=jnp.int32)
    shifts = jnp.stack([(slot_ids // 9 - 1) * LX, (slot_ids // 3 % 3 - 1) * LY, (slot_ids % 3 - 1) * DEPTH], axis=1).astype(jnp.float32)
    return (shifts, slot_ids == 13)

def wrap_pad(array):
    return jnp.pad(array, ((0, 0), (1, 1), (1, 1), (1, 1), (0, 0)), mode='wrap')

def neighbourhood(padded, flat_index):
    channels = padded.shape[0]
    atom_count = padded.shape[-1]
    index_x = flat_index // (N_GY * N_GZ)
    index_y = flat_index // N_GZ % N_GY
    index_z = flat_index % N_GZ
    zero = jnp.zeros((), jnp.int32)
    block = lax.dynamic_slice(padded, (zero, index_x, index_y, index_z, zero), (channels, 3, 3, 3, atom_count))
    return block.reshape(channels, 27, atom_count).transpose(1, 0, 2)

def reference(positions, polarizability, direct_field, groups):
    full_shape = positions.shape
    frame = jnp.concatenate([positions, polarizability[None]], axis=0)
    padded_frame = wrap_pad(frame)
    own_pos_all = positions.reshape(3, DEVICES, -1)
    polar = polarizability.reshape(DEVICES, -1)
    group_all = groups.reshape(DEVICES, -1)
    direct = direct_field.reshape(3, DEVICES, -1)
    shifts, centre_flags = slot_table()
    flat_ids = jnp.arange(DEVICES, dtype=jnp.int32)

    def local_frame(flat_index):
        slots = neighbourhood(padded_frame, flat_index)
        return (slots[:, :3] + shifts[:, :, None], slots[:, 3])

    def apply_all(vector):
        padded_vec = wrap_pad(vector.reshape(full_shape))

        def one_device(flat_index):
            far_pos, far_polar = local_frame(flat_index)
            return apply_tensor(own_pos_all[:, flat_index], polar[flat_index], group_all[flat_index], far_pos, far_polar, neighbourhood(padded_vec, flat_index), centre_flags)
        return lax.map(one_device, flat_ids).transpose(1, 0, 2)
    dipole_start = polar * direct
    resid_start = apply_all(dipole_start)
    precond_start = polar * resid_start
    search_first = precond_start
    norm_first = jnp.sum(resid_start * precond_start)
    image_first = search_first / polar - apply_all(search_first)
    gamma_first = norm_first / jnp.sum(search_first * image_first)
    dipole_mid = dipole_start + gamma_first * search_first
    resid_mid = resid_start - gamma_first * image_first
    precond_mid = polar * resid_mid
    norm_mid = jnp.sum(resid_mid * precond_mid)
    search_second = precond_mid + norm_mid / norm_first * search_first
    image_second = search_second / polar - apply_all(search_second)
    gamma_second = norm_mid / jnp.sum(search_second * image_second)
    dipoles = dipole_mid + gamma_second * search_second
    energy = -jnp.sum(dipoles * direct) / (2.0 * ATOMS)
    adjoint = polar * direct + polar * apply_all(dipoles)
    padded_dip = wrap_pad(dipoles.reshape(full_shape))
    padded_adj = wrap_pad(adjoint.reshape(full_shape))

    def grad_device(flat_index):
        far_pos, far_polar = local_frame(flat_index)
        return pair_gradient(own_pos_all[:, flat_index], polar[flat_index], group_all[flat_index], far_pos, far_polar, dipoles[:, flat_index], adjoint[:, flat_index], neighbourhood(padded_dip, flat_index), neighbourhood(padded_adj, flat_index), centre_flags)
    gradient = lax.map(grad_device, flat_ids).transpose(1, 0, 2)
    return (dipoles.reshape(full_shape), gradient.reshape(full_shape), energy)
```

```python
import numpy as np

import jax
import jax.numpy as jnp
from jax import lax
from jax.experimental import pallas as pl
from jax.experimental.pallas import tpu as pltpu
from jax.sharding import PartitionSpec as P

LX = 8
LY = 8
DEPTH = 3
CUTOFF = 3
LAYERS = 4
FULL_Z = DEPTH * LAYERS
HALO = 2 * CUTOFF
WIDE = LX + 2 * HALO
ATOMS = LX * LY * DEPTH
ROWS = 24
LANES = 512
BLOCKS = 3
JITTER = 0.4

thole_factor = 0.39
group_scale = 0.5


def within(dx, dy, dz):
    least = sum(max(abs(o) - JITTER, 0.0) ** 2 for o in (dx, dy, dz))
    return least < CUTOFF * CUTOFF


def half_offsets():
    reach = range(-CUTOFF, CUTOFF + 1)
    columns = []
    count = 0
    for dx in range(0, CUTOFF + 1):
        for dy in reach:
            depths = [
                dz
                for dz in reach
                if (dx > 0 or dy > 0 or (dy == 0 and dz > 0)) and within(dx, dy, dz)
            ]
            if depths:
                columns.append((dx, dy, depths, count))
                count += len(depths)
    return columns, count


COLUMNS, OFFSETS = half_offsets()


def may_share_group(dx, dy, dz):
    return dx == 0 and abs(DEPTH * dy + dz) <= 7 and abs(dz) < DEPTH


def lane_iota(rows=ROWS):
    return lax.broadcasted_iota(jnp.int32, (rows, 128), 1)


def shifted(source, field, shift, out, slot):
    if shift == 0:
        for b in range(BLOCKS):
            out[slot, b] = source[field, b]
        return
    keep = lane_iota() < 128 - shift
    turned = [pltpu.roll(source[field, b], 128 - shift, 1) for b in range(BLOCKS + 1)]
    for b in range(BLOCKS):
        out[slot, b] = jnp.where(keep, turned[b], turned[b + 1])


def spread(values, block_rows, total):
    shift = block_rows
    for c in range(3):
        if shift == 0:
            for b in range(BLOCKS):
                total[c, b, 12:36] += values[c, b]
            continue
        keep = lane_iota() >= shift
        turned = [pltpu.roll(values[c, b], shift, 1) for b in range(BLOCKS)]
        for b in range(BLOCKS):
            if b == 0:
                total[c, b, 12:36] += jnp.where(keep, turned[b], 0.0)
            else:
                total[c, b, 12:36] += jnp.where(keep, turned[b], turned[b - 1])


def row_limit(v):
    if v == 0:
        return jnp.ones((8, 128), jnp.float32)
    row = lax.broadcasted_iota(jnp.int32, (8, 128), 0)
    return jnp.where(row < FULL_Z - 8, 1.0, -1.0e3)


def finish(polar_of, own_sum, partner_sum, ring, out):
    for c in range(3):
        for b in range(BLOCKS):
            folded = (
                own_sum[c, b, 0:12]
                + partner_sum[c, b, 15:27]
                + partner_sum[c, b, 27:39]
                + partner_sum[c, b, 3:15]
            )
            value = folded * polar_of(b)
            ring[3:15] = value
            ring[15:27] = value
            ring[27:39] = value
            out[c, b] = ring[12:36]
        out[c, BLOCKS] = jnp.zeros((ROWS, 128), jnp.float32)


def own_lanes(b):
    lane = lax.broadcasted_iota(jnp.int32, (12, 128), 1) + 128 * b
    x = lane // WIDE
    y = lane - x * WIDE
    return (x >= HALO) & (x < HALO + LX) & (y >= HALO) & (y < HALO + LY)


def inner(first, second, inverse_of):
    total = jnp.zeros((12, 128), jnp.float32)
    for b in range(BLOCKS):
        dot = sum(first[c, b, 3:15] * second[c, b, 3:15] for c in range(3))
        total = total + jnp.where(own_lanes(b), dot * inverse_of(b), 0.0)
    return jnp.sum(total)


def apply_pass(vec, spots, spots_far, c3_ref, c5_ref, far, own_sum, partner, partner_sum):
    own_sum[...] = jnp.zeros_like(own_sum)
    partner_sum[...] = jnp.zeros_like(partner_sum)
    for number, (dx, dy, depths, first) in enumerate(COLUMNS):
        shift = dx * WIDE + dy
        for c in range(3):
            shifted(vec, c, shift, far, c)
        partner[...] = jnp.zeros_like(partner)

        def per_block(b, carry):
            for v in range(2):
                rows = pl.ds(3 + 8 * v, 8)
                own = [spots[c, b, rows, :] for c in range(3)]
                own_u = [vec[c, b, rows, :] for c in range(3)]
                acc = [own_sum[c, b, pl.ds(8 * v, 8), :] for c in range(3)]
                for n, dz in enumerate(depths):
                    far_rows = pl.ds(3 + dz + 8 * v, 8)
                    d = [spots_far[number, c, b, far_rows, :] - own[c] for c in range(3)]
                    far_u = [far[c, b, far_rows, :] for c in range(3)]
                    c3 = c3_ref[first + n, b, pl.ds(8 * v, 8), :]
                    c5 = c5_ref[first + n, b, pl.ds(8 * v, 8), :]
                    along_far = c5 * (d[0] * far_u[0] + d[1] * far_u[1] + d[2] * far_u[2])
                    along_own = c5 * (d[0] * own_u[0] + d[1] * own_u[1] + d[2] * own_u[2])
                    for c in range(3):
                        acc[c] = acc[c] + (along_far * d[c] - c3 * far_u[c])
                        partner[c, b, far_rows, :] += along_own * d[c] - c3 * own_u[c]
                for c in range(3):
                    own_sum[c, b, pl.ds(8 * v, 8), :] = acc[c]
            return carry

        lax.fori_loop(0, BLOCKS, per_block, 0)
        spread(partner, shift, partner_sum)


def first_kernel(
    base_ref, c3_ref, c5_ref, spots_far, u1_ref, u2_ref, moment_ref,
    fields, far, own_sum, partner, partner_sum, ring, vec, vec_b,
):
    for b in range(BLOCKS + 1):
        lanes = slice(128 * b, 128 * b + 128)
        for f in range(3):
            fields[f, b] = base_ref[f, :, lanes]
            vec[f, b] = base_ref[4 + f, :, lanes]
        polar = base_ref[3, :, lanes]
        fields[3, b] = (thole_factor**0.5) * lax.rsqrt(polar)
        fields[4, b] = base_ref[7, :, lanes]
        fields[5, b] = polar
    polar_of = lambda b: fields[5, b, 3:15]
    inverse_of = lambda b: 1.0 / fields[5, b, 3:15]

    own_sum[...] = jnp.zeros_like(own_sum)
    partner_sum[...] = jnp.zeros_like(partner_sum)
    for number, (dx, dy, depths, first) in enumerate(COLUMNS):
        shift = dx * WIDE + dy
        for c in range(3):
            shifted(fields, c, shift, spots_far.at[number], c)
            shifted(vec, c, shift, far, c)
        shifted(fields, 3, shift, far, 3)
        if dx == 0:
            shifted(fields, 4, shift, far, 4)
        partner[...] = jnp.zeros_like(partner)

        def per_block(b, carry):
            for v in range(2):
                rows = pl.ds(3 + 8 * v, 8)
                own = [fields[c, b, rows, :] for c in range(3)]
                root = fields[3, b, rows, :]
                own_u = [vec[c, b, rows, :] for c in range(3)]
                limit = row_limit(v)
                acc = [own_sum[c, b, pl.ds(8 * v, 8), :] for c in range(3)]
                for n, dz in enumerate(depths):
                    far_rows = pl.ds(3 + dz + 8 * v, 8)
                    d = [spots_far[number, c, b, far_rows, :] - own[c] for c in range(3)]
                    far_u = [far[c, b, far_rows, :] for c in range(3)]
                    s = d[0] * d[0] + d[1] * d[1] + d[2] * d[2]
                    inv = lax.rsqrt(s)
                    inv2 = inv * inv
                    inv3 = inv2 * inv
                    x = (s * s * inv) * (root * far[3, b, far_rows, :])
                    e = jnp.exp(-x)
                    l3 = 1.0 - e
                    l5 = l3 - x * e
                    cut = jnp.maximum(limit - s * (1.0 / (CUTOFF * CUTOFF)), 0.0)
                    weight = cut * cut * inv3
                    if may_share_group(dx, dy, dz):
                        same = fields[4, b, rows, :] == far[4, b, far_rows, :]
                        weight = jnp.where(same, group_scale * weight, weight)
                    c3 = weight * l3
                    c5 = (3.0 * weight) * (inv2 * l5)
                    c3_ref[first + n, b, pl.ds(8 * v, 8), :] = c3
                    c5_ref[first + n, b, pl.ds(8 * v, 8), :] = c5
                    along_far = c5 * (d[0] * far_u[0] + d[1] * far_u[1] + d[2] * far_u[2])
                    along_own = c5 * (d[0] * own_u[0] + d[1] * own_u[1] + d[2] * own_u[2])
                    for c in range(3):
                        acc[c] = acc[c] + (along_far * d[c] - c3 * far_u[c])
                        partner[c, b, far_rows, :] += along_own * d[c] - c3 * own_u[c]
                for c in range(3):
                    own_sum[c, b, pl.ds(8 * v, 8), :] = acc[c]
            return carry

        lax.fori_loop(0, BLOCKS, per_block, 0)
        spread(partner, shift, partner_sum)
    finish(polar_of, own_sum, partner_sum, ring, vec_b)
    moments = [inner(vec, vec, inverse_of), inner(vec, vec_b, inverse_of), inner(vec_b, vec_b, inverse_of)]
    for c in range(3):
        for b in range(BLOCKS + 1):
            u1_ref[c, :, 128 * b : 128 * b + 128] = vec_b[c, b]
    apply_pass(vec_b, fields, spots_far, c3_ref, c5_ref, far, own_sum, partner, partner_sum)
    finish(polar_of, own_sum, partner_sum, ring, vec)
    moments += [inner(vec_b, vec, inverse_of), inner(vec, vec, inverse_of)]
    for c in range(3):
        for b in range(BLOCKS):
            u2_ref[c, :, 128 * b : 128 * b + 128] = vec[c, b, 3:15]
    lane = lax.broadcasted_iota(jnp.int32, (1, 128), 1)
    row = jnp.zeros((1, 128), jnp.float32)
    for n, value in enumerate(moments):
        row = jnp.where(lane == n, value, row)
    moment_ref[...] = row


def second_kernel(
    base_ref, c3_ref, c5_ref, spots_far, u2_ref, moment_in, u3_ref, moment_ref,
    fields, far, own_sum, partner, partner_sum, ring, vec, vec_b,
):
    for b in range(BLOCKS + 1):
        lanes = slice(128 * b, 128 * b + 128)
        for f in range(3):
            fields[f, b] = base_ref[f, :, lanes]
            vec[f, b] = u2_ref[f, :, lanes]
        fields[3, b] = base_ref[3, :, lanes]
    polar_of = lambda b: fields[3, b, 3:15]
    inverse_of = lambda b: 1.0 / fields[3, b, 3:15]
    apply_pass(vec, fields, spots_far, c3_ref, c5_ref, far, own_sum, partner, partner_sum)
    finish(polar_of, own_sum, partner_sum, ring, vec_b)
    for c in range(3):
        for b in range(BLOCKS + 1):
            u3_ref[c, :, 128 * b : 128 * b + 128] = vec_b[c, b]
    lane = lax.broadcasted_iota(jnp.int32, (1, 128), 1)
    moment_ref[...] = jnp.where(lane == 5, inner(vec, vec_b, inverse_of), moment_in[...])


def gradient_kernel(moment_ref, own_ref, far_ref, out_ref, energy_ref):
    total = jnp.sum(moment_ref[...], axis=0, keepdims=True)
    lane = lax.broadcasted_iota(jnp.int32, (1, 128), 1)

    def pick(n):
        return jnp.sum(jnp.where(lane == n, total, 0.0), axis=1, keepdims=True)

    m0, m1, m2, m3, m4, m5 = (pick(n) for n in range(6))
    g = m2 / (m2 - m3)
    rest = 1.0 - g
    rz1 = rest * rest * m2 + 2.0 * g * rest * m3 + g * g * m4
    a = rest + rz1 / m2
    curve = a * a * (m2 - m3) + 2.0 * a * g * (m3 - m4) + g * g * (m4 - m5)
    g1 = rz1 / curve
    k1 = g + g1 * a
    k2 = g1 * g
    energy_ref[...] = -(m0 + k1 * m1 + k2 * m2)
    far_k1 = jnp.broadcast_to(k1, (1, 128))
    far_k2 = jnp.broadcast_to(k2, (1, 128))

    def plane(x, carry):
        far = []
        for n in range(2 * CUTOFF + 1):
            block = far_ref[x + n]
            spot = [block[c : c + 1] for c in range(5)]
            u = [[block[5 + 3 * q + c : 6 + 3 * q + c] for c in range(3)] for q in range(4)]
            dip = [u[0][c] + far_k1 * u[1][c] + far_k2 * u[2][c] for c in range(3)]
            adj = [u[0][c] + u[1][c] + far_k1 * u[2][c] + far_k2 * u[3][c] for c in range(3)]
            far.append((spot, dip, adj))
        for t in range(LY * DEPTH // 8):
            start = pl.multiple_of(x * (LY * DEPTH) + 8 * t, 8)
            own_block = own_ref[pl.ds(start, 8), :]

            def own_field(n):
                return jnp.broadcast_to(own_block[:, n : n + 1], (8, 128))

            spot_i = [own_field(c) for c in range(5)]
            u = [[own_field(5 + 3 * q + c) for c in range(3)] for q in range(4)]
            dip_i = [u[0][c] + k1 * u[1][c] + k2 * u[2][c] for c in range(3)]
            adj_i = [u[0][c] + u[1][c] + k1 * u[2][c] + k2 * u[3][c] for c in range(3)]
            acc = [jnp.zeros((8, 128), jnp.float32) for _ in range(3)]
            for n in range(2 * CUTOFF + 1):
                spot, dip, adj = far[n]
                d = [spot[c] - spot_i[c] for c in range(3)]
                s = d[0] * d[0] + d[1] * d[1] + d[2] * d[2]
                if n == CUTOFF:
                    own_atom = s == 0.0
                    s = jnp.where(own_atom, 1.0, s)
                inv = lax.rsqrt(s)
                inv2 = inv * inv
                x_damp = (s * s * inv) * (spot_i[3] * spot[3])
                xe = x_damp * jnp.exp(-x_damp)
                e = jnp.exp(-x_damp)
                l3 = 1.0 - e
                l5 = l3 - xe
                cut = jnp.maximum(1.0 - s * (1.0 / (CUTOFF * CUTOFF)), 0.0)
                scale = inv2 * inv
                if n == CUTOFF:
                    scale = jnp.where(spot[4] == spot_i[4], group_scale * scale, scale)
                    scale = jnp.where(own_atom, 0.0, scale)
                ratio = cut * inv2
                scale = scale * cut
                scale5 = 3.0 * scale * inv2
                c5 = scale5 * cut * l5
                slope3 = scale * ((-4.0 / (CUTOFF * CUTOFF)) * l3 - 3.0 * ratio * l5)
                slope5 = scale5 * (
                    (-4.0 / (CUTOFF * CUTOFF)) * l5 + ratio * (3.0 * x_damp * xe - 5.0 * l5)
                )
                own_dip = d[0] * dip_i[0] + d[1] * dip_i[1] + d[2] * dip_i[2]
                own_adj = d[0] * adj_i[0] + d[1] * adj_i[1] + d[2] * adj_i[2]
                far_dip = d[0] * dip[0] + d[1] * dip[1] + d[2] * dip[2]
                far_adj = d[0] * adj[0] + d[1] * adj[1] + d[2] * adj[2]
                cross = (
                    dip_i[0] * adj[0] + dip_i[1] * adj[1] + dip_i[2] * adj[2]
                    + adj_i[0] * dip[0] + adj_i[1] * dip[1] + adj_i[2] * dip[2]
                )
                radial = slope5 * (own_dip * far_adj + own_adj * far_dip) - slope3 * cross
                p1, p2, p3, p4 = c5 * own_dip, c5 * far_adj, c5 * own_adj, c5 * far_dip
                for c in range(3):
                    acc[c] = acc[c] + (
                        radial * d[c] + p1 * adj[c] + p2 * dip_i[c] + p3 * dip[c] + p4 * adj_i[c]
                    )
            lanes = lax.broadcasted_iota(jnp.int32, (8, 128), 1)
            result = jnp.zeros((8, 128), jnp.float32)
            for c in range(3):
                result = jnp.where(lanes == c, dip_i[c], result)
                force = -0.5 * jnp.sum(acc[c], axis=1, keepdims=True)
                result = jnp.where(lanes == 3 + c, force, result)
            out_ref[pl.ds(start, 8), :] = result
        return carry

    lax.fori_loop(0, LX, plane, 0)


def vmem_specs(count):
    return [pl.BlockSpec(memory_space=pltpu.VMEM)] * count


F32 = jnp.float32
SCRATCH = [
    pltpu.VMEM((6, BLOCKS + 1, ROWS, 128), F32),
    pltpu.VMEM((5, BLOCKS, ROWS, 128), F32),
    pltpu.VMEM((3, BLOCKS, 16, 128), F32),
    pltpu.VMEM((3, BLOCKS, ROWS, 128), F32),
    pltpu.VMEM((3, BLOCKS, 48, 128), F32),
    pltpu.VMEM((48, 128), F32),
    pltpu.VMEM((3, BLOCKS + 1, ROWS, 128), F32),
    pltpu.VMEM((3, BLOCKS + 1, ROWS, 128), F32),
]
COUPLING = jax.ShapeDtypeStruct((OFFSETS, BLOCKS, 16, 128), F32)
PARAMS = pltpu.CompilerParams(vmem_limit_bytes=40 * 1024 * 1024)


def run_first(base):
    outs = (
        COUPLING,
        COUPLING,
        jax.ShapeDtypeStruct((len(COLUMNS), 3, BLOCKS, ROWS, 128), F32),
        jax.ShapeDtypeStruct((3, ROWS, LANES), F32),
        jax.ShapeDtypeStruct((3, FULL_Z, 128 * BLOCKS), F32),
        jax.ShapeDtypeStruct((1, 128), F32),
    )
    return pl.pallas_call(
        first_kernel,
        out_shape=outs,
        in_specs=vmem_specs(1),
        out_specs=tuple(vmem_specs(len(outs))),
        scratch_shapes=SCRATCH,
        compiler_params=PARAMS,
    )(base)


def run_second(base, c3, c5, spots_far, u2, moments):
    outs = (jax.ShapeDtypeStruct((3, ROWS, LANES), F32), jax.ShapeDtypeStruct((1, 128), F32))
    return pl.pallas_call(
        second_kernel,
        out_shape=outs,
        in_specs=vmem_specs(6),
        out_specs=tuple(vmem_specs(2)),
        scratch_shapes=SCRATCH,
        compiler_params=PARAMS,
    )(base, c3, c5, spots_far, u2, moments)


def run_gradient(moments, own, far):
    return pl.pallas_call(
        gradient_kernel,
        out_shape=(
            jax.ShapeDtypeStruct((ATOMS, 128), F32),
            jax.ShapeDtypeStruct((1, 1), F32),
        ),
        in_specs=vmem_specs(3),
        out_specs=tuple(vmem_specs(2)),
        compiler_params=PARAMS,
    )(moments, own, far)


def both_sides(low, high, axis):
    count = lax.axis_size(axis)
    below = lax.ppermute(high, axis, [(i, (i + 1) % count) for i in range(count)])
    above = lax.ppermute(low, axis, [((i + 1) % count, i) for i in range(count)])
    return below, above


def widen(lattice):
    lead = lattice.shape[:-2]
    low = lattice[..., :HALO].reshape(*lead, LX * HALO)
    high = lattice[..., LY - HALO :].reshape(*lead, LX * HALO)
    below, above = both_sides(low, high, "gy")
    along_y = jnp.concatenate(
        [below.reshape(*lead, LX, HALO), lattice, above.reshape(*lead, LX, HALO)], axis=-1
    ).reshape(*lead, LX * WIDE)
    below, above = both_sides(
        along_y[..., : HALO * WIDE], along_y[..., (LX - HALO) * WIDE :], "gx"
    )
    flat = jnp.concatenate([below, along_y, above], axis=-1)
    flat = jnp.pad(flat, [(0, 0)] * len(lead) + [(0, LANES - WIDE * WIDE)])
    return jnp.concatenate([flat[:, FULL_Z - CUTOFF :], flat, flat[:, : ROWS - FULL_Z - CUTOFF]], axis=1)


def frame_constants():
    lane = np.arange(LANES)
    x, y = lane // WIDE, lane % WIDE
    row = np.arange(ROWS)
    full = np.zeros((8, ROWS, LANES), np.float32)
    full[0] = (x - HALO)[None, :]
    full[1] = (y - HALO)[None, :]
    full[2] = (row - CUTOFF)[:, None]
    full[3] = np.where(lane >= WIDE * WIDE, 0.05, 0.0)[None, :]
    domain = (x + 2) // LX * 8 + (y + 2) // LY
    layer = (row - CUTOFF) % FULL_Z // DEPTH
    full[7] = 64.0 * (domain[None, :] * LAYERS + layer[:, None])
    return full


def on_device(positions, polarizability, direct_field, groups):
    site = np.arange(ATOMS)
    lattice = np.stack([site // (LY * DEPTH), site // DEPTH % LY, site % DEPTH]).astype(np.float32)
    polar = polarizability.reshape(1, ATOMS)
    start = polar * direct_field.reshape(3, ATOMS)
    packed = jnp.concatenate(
        [positions.reshape(3, ATOMS) - lattice, polar, start, groups.reshape(1, ATOMS).astype(F32)]
    )
    column = packed.reshape(8, LX * LY, DEPTH).transpose(0, 2, 1)
    layer = lax.axis_index("gz")
    copies = jnp.broadcast_to(column[None], (LAYERS, *column.shape))
    column = lax.all_to_all(copies, "gz", 0, 0).transpose(1, 0, 2, 3)
    base = widen(column.reshape(8, FULL_Z, LX, LY)) + frame_constants()
    c3, c5, spots_far, u1, u2, moments = run_first(base)
    own_u2 = u2[..., HALO * WIDE : (HALO + LX) * WIDE].reshape(3, FULL_Z, LX, WIDE)
    u2_wide = widen(own_u2[..., HALO : HALO + LY])
    u3, moments = run_second(base, c3, c5, spots_far, u2_wide, moments)
    for axis in ("gx", "gy"):
        count = lax.axis_size(axis)
        copies = jnp.broadcast_to(moments[None], (count, 1, 128))
        moments = lax.all_to_all(copies, axis, 0, 0).reshape(count, 128)
        if axis == "gx":
            moments = jnp.sum(moments, axis=0, keepdims=True)
    root = (thole_factor**0.5) * lax.rsqrt(base[3:4])
    everything = jnp.concatenate([base[:3], root, base[7:8], base[4:7], u1, u2_wide, u3])
    nearby = lax.dynamic_slice_in_dim(everything, layer * DEPTH, DEPTH + 2 * CUTOFF, axis=1)
    nearby = nearby[..., : WIDE * WIDE].reshape(-1, DEPTH + 2 * CUTOFF, WIDE, WIDE)
    inside = slice(HALO - CUTOFF, HALO + LX + CUTOFF)
    nearby = nearby[:, :, inside, inside]
    own = nearby[:, CUTOFF:-CUTOFF, CUTOFF:-CUTOFF, CUTOFF:-CUTOFF]
    own = own.transpose(2, 3, 1, 0).reshape(ATOMS, -1)
    far = nearby.transpose(2, 0, 3, 1).reshape(LX + 2 * CUTOFF, nearby.shape[0], -1)
    far = jnp.pad(far, ((0, 0), (0, 0), (0, 128 - far.shape[-1])), constant_values=1.0e3)
    out, energy = run_gradient(moments, own, far)
    out = out[:, :6].T
    devices = lax.axis_size("gx") * lax.axis_size("gy") * lax.axis_size("gz")
    return (
        out[:3].reshape(3, 1, 1, 1, ATOMS),
        out[3:].reshape(3, 1, 1, 1, ATOMS),
        (energy / (2.0 * ATOMS * devices)).reshape(()),
    )


def solution(mesh):
    along = ("gx", "gy", "gz", None)
    return jax.shard_map(
        on_device,
        mesh=mesh,
        in_specs=(P(None, *along), P(*along), P(None, *along), P(*along)),
        out_specs=(P(None, *along), P(None, *along), P()),
        check_vma=False,
    )
```

```python
import numpy as np

import jax
import jax.numpy as jnp
from jax import lax
from jax.experimental import pallas as pl
from jax.experimental.pallas import tpu as pltpu
from jax.sharding import PartitionSpec as P

LX = 8
LY = 8
DEPTH = 3
CUTOFF = 3
LAYERS = 4
FULL_Z = DEPTH * LAYERS
HALO = 2 * CUTOFF
WIDE = LX + 2 * HALO
ATOMS = LX * LY * DEPTH
ROWS = 24
LANES = 512
HALF = FULL_Z // 2
LEVELS = HALF + 2 * CUTOFF
JITTER = 0.4
SPAN_X = LX + 2 * CUTOFF
SPAN_Y = LY + 2 * CUTOFF
SPAN_Z = DEPTH + 2 * CUTOFF
FIELDS = 17

thole_factor = 0.39
group_scale = 0.5


def within(dx, dy, dz):
    least = sum(max(abs(o) - JITTER, 0.0) ** 2 for o in (dx, dy, dz))
    return least < CUTOFF * CUTOFF


def half_offsets():
    reach = range(-CUTOFF, CUTOFF + 1)
    columns = []
    count = 0
    for dx in range(0, CUTOFF + 1):
        for dy in reach:
            depths = [
                dz
                for dz in reach
                if (dx > 0 or dy > 0 or (dy == 0 and dz > 0)) and within(dx, dy, dz)
            ]
            if depths:
                columns.append((dx, dy, depths, count))
                count += len(depths)
    return columns, count


COLUMNS, OFFSETS = half_offsets()


def may_share_group(dx, dy, dz):
    return dx == 0 and abs(DEPTH * dy + dz) <= 7 and abs(dz) < DEPTH


def lane_iota(rows=8):
    return lax.broadcasted_iota(jnp.int32, (rows, 128), 1)


def wrap_levels(value_of, out, slot, lift=0.0):
    for level in range(HALF):
        value = value_of(level)
        out[slot, CUTOFF + level] = value
        if level < CUTOFF:
            out[slot, CUTOFF + HALF + level] = pltpu.roll(value, 4, 0) + lift * HALF
        if level >= HALF - CUTOFF:
            out[slot, CUTOFF - HALF + level] = pltpu.roll(value, 4, 0) - lift * HALF


def shifted(source, field, shift, out, slot):
    if shift == 0:
        for level in range(LEVELS):
            out[slot, level] = source[field, level]
        return
    keep = lane_iota() >= shift
    for level in range(LEVELS):
        here = source[field, level]
        both = jnp.where(keep, here, pltpu.roll(here, 7, 0))
        out[slot, level] = pltpu.roll(both, 128 - shift, 1)


def spread(values, depths, shift, total):
    keep = lane_iota() >= shift
    for c in range(3):
        for level in range(-CUTOFF, HALF + CUTOFF):
            shares = [
                values[n, c, level - dz] for n, dz in enumerate(depths) if 0 <= level - dz < HALF
            ]
            if not shares:
                continue
            while len(shares) > 1:
                shares = [sum(shares[i : i + 2]) for i in range(0, len(shares), 2)]
            part = shares[0]
            if shift:
                turned = pltpu.roll(part, shift, 1)
                part = jnp.where(keep, turned, pltpu.roll(turned, 1, 0))
            total[c, CUTOFF + level] += part


def finish(polar_of, own_sum, partner_sum, out):
    for c in range(3):

        def value_of(level):
            other = CUTOFF + level + (HALF if level < CUTOFF else -HALF)
            folded = own_sum[c, level] + partner_sum[c, CUTOFF + level]
            return (folded + pltpu.roll(partner_sum[c, other], 4, 0)) * polar_of(level)

        wrap_levels(value_of, out, c)


def own_places():
    block = lax.broadcasted_iota(jnp.int32, (8, 128), 0)
    place = lane_iota() + 128 * jnp.where(block >= 4, block - 4, block)
    x = place // WIDE
    y = place - x * WIDE
    return (x >= HALO) & (x < HALO + LX) & (y >= HALO) & (y < HALO + LY)


def inner(first, second, inverse_of):
    total = jnp.zeros((8, 128), jnp.float32)
    for level in range(HALF):
        at = CUTOFF + level
        total = total + sum(first[c, at] * second[c, at] for c in range(3)) * inverse_of(level)
    return jnp.sum(jnp.where(own_places(), total, 0.0))


def apply_pass(vec, spots, spots_far, c3_ref, c5_ref, far, own_sum, partner, partner_sum):
    own_sum[...] = jnp.zeros_like(own_sum)
    partner_sum[...] = jnp.zeros_like(partner_sum)
    for number, (dx, dy, depths, first) in enumerate(COLUMNS):
        shift = dx * WIDE + dy
        for c in range(3):
            shifted(vec, c, shift, far, c)

        def per_level(level, carry):
            own = [spots[c, CUTOFF + level] for c in range(3)]
            own_u = [vec[c, CUTOFF + level] for c in range(3)]
            acc = [own_sum[c, level] for c in range(3)]
            for n, dz in enumerate(depths):
                at = CUTOFF + dz + level
                d = [spots_far[number, c, at] - own[c] for c in range(3)]
                far_u = [far[c, at] for c in range(3)]
                c3 = c3_ref[first + n, level]
                c5 = c5_ref[first + n, level]
                along_far = c5 * (d[0] * far_u[0] + d[1] * far_u[1] + d[2] * far_u[2])
                along_own = c5 * (d[0] * own_u[0] + d[1] * own_u[1] + d[2] * own_u[2])
                for c in range(3):
                    acc[c] = acc[c] + (along_far * d[c] - c3 * far_u[c])
                    partner[n, c, level] = along_own * d[c] - c3 * own_u[c]
            for c in range(3):
                own_sum[c, level] = acc[c]
            return carry

        lax.fori_loop(0, HALF, per_level, 0, unroll=2)
        spread(partner, depths, shift, partner_sum)


def pack_kernel(spot_ref, polar_ref, direct_ref, group_ref, out_ref, rows):
    site = lax.broadcasted_iota(jnp.int32, (1, ATOMS), 1)
    x = site // (LY * DEPTH)
    y = site // DEPTH - LY * x
    z = site - DEPTH * (site // DEPTH)
    for c, lattice in enumerate((x, y, z)):
        rows[c : c + 1] = spot_ref[c, 0, 0] - lattice.astype(jnp.float32)
        rows[4 + c : 5 + c] = polar_ref[0, 0] * direct_ref[c, 0, 0]
    rows[3:4] = polar_ref[0, 0]
    rows[7:8] = group_ref[0, 0].astype(jnp.float32)
    old = lax.broadcasted_iota(jnp.int32, (ATOMS, ATOMS), 0)
    new = lax.broadcasted_iota(jnp.int32, (ATOMS, ATOMS), 1)
    plane = new // (LX * LY)
    order = jnp.where(old == DEPTH * (new - LX * LY * plane) + plane, 1.0, 0.0)
    packed = jnp.dot(
        rows[...], order, precision=lax.Precision.HIGHEST, preferred_element_type=jnp.float32
    )
    for n in range(LAYERS):
        out_ref[n] = packed


def first_kernel(
    base_ref, c3_ref, c5_ref, u1_ref, u2_ref, moment_ref,
    fields, far, own_sum, partner, partner_sum, vec, vec_b, spots_far,
):
    for f in range(3):
        wrap_levels(lambda level: base_ref[f, level], fields, f, 1.0 if f == 2 else 0.0)
        wrap_levels(lambda level: base_ref[4 + f, level], vec, f)
    wrap_levels(lambda level: (thole_factor**0.5) * lax.rsqrt(base_ref[3, level]), fields, 3)
    wrap_levels(lambda level: base_ref[7, level], fields, 4)
    polar_of = lambda level: base_ref[3, level]
    inverse_of = lambda level: 1.0 / base_ref[3, level]

    own_sum[...] = jnp.zeros_like(own_sum)
    partner_sum[...] = jnp.zeros_like(partner_sum)
    for number, (dx, dy, depths, first) in enumerate(COLUMNS):
        shift = dx * WIDE + dy
        for c in range(3):
            shifted(fields, c, shift, spots_far.at[number], c)
            shifted(vec, c, shift, far, c)
        shifted(fields, 3, shift, far, 3)
        if dx == 0:
            shifted(fields, 4, shift, far, 4)

        def per_level(level, carry):
            own = [fields[c, CUTOFF + level] for c in range(3)]
            root = fields[3, CUTOFF + level]
            own_u = [vec[c, CUTOFF + level] for c in range(3)]
            acc = [own_sum[c, level] for c in range(3)]
            for n, dz in enumerate(depths):
                at = CUTOFF + dz + level
                d = [spots_far[number, c, at] - own[c] for c in range(3)]
                far_u = [far[c, at] for c in range(3)]
                s = d[0] * d[0] + d[1] * d[1] + d[2] * d[2]
                inv = lax.rsqrt(s)
                inv2 = inv * inv
                inv3 = inv2 * inv
                x = (s * s * inv) * (root * far[3, at])
                e = jnp.exp(-x)
                l3 = 1.0 - e
                l5 = l3 - x * e
                cut = jnp.maximum(1.0 - s * (1.0 / (CUTOFF * CUTOFF)), 0.0)
                weight = cut * cut * inv3
                if may_share_group(dx, dy, dz):
                    same = fields[4, CUTOFF + level] == far[4, at]
                    weight = jnp.where(same, group_scale * weight, weight)
                c3 = weight * l3
                c5 = (3.0 * weight) * (inv2 * l5)
                c3_ref[first + n, level] = c3
                c5_ref[first + n, level] = c5
                along_far = c5 * (d[0] * far_u[0] + d[1] * far_u[1] + d[2] * far_u[2])
                along_own = c5 * (d[0] * own_u[0] + d[1] * own_u[1] + d[2] * own_u[2])
                for c in range(3):
                    acc[c] = acc[c] + (along_far * d[c] - c3 * far_u[c])
                    partner[n, c, level] = along_own * d[c] - c3 * own_u[c]
            for c in range(3):
                own_sum[c, level] = acc[c]
            return carry

        lax.fori_loop(0, HALF, per_level, 0, unroll=2)
        spread(partner, depths, shift, partner_sum)
    finish(polar_of, own_sum, partner_sum, vec_b)
    moments = [inner(vec, vec, inverse_of), inner(vec, vec_b, inverse_of), inner(vec_b, vec_b, inverse_of)]
    for c in range(3):
        for level in range(HALF):
            u1_ref[c, level] = vec_b[c, CUTOFF + level]
    apply_pass(vec_b, fields, spots_far, c3_ref, c5_ref, far, own_sum, partner, partner_sum)
    finish(polar_of, own_sum, partner_sum, vec)
    moments += [inner(vec_b, vec, inverse_of), inner(vec, vec, inverse_of)]
    for c in range(3):
        for level in range(HALF):
            u2_ref[c, level] = vec[c, CUTOFF + level]
    lane = lax.broadcasted_iota(jnp.int32, (1, 128), 1)
    row = jnp.zeros((1, 128), jnp.float32)
    for n, value in enumerate(moments):
        row = jnp.where(lane == n, value, row)
    moment_ref[...] = row


def lay_planes(layer, base_ref, u1_ref, u2_ref, u3, stage, far_ref):
    lane = lane_iota(ROWS)
    row = lax.broadcasted_iota(jnp.int32, (ROWS, 128), 0)
    for z in range(-CUTOFF, FULL_Z + CUTOFF):
        half, level = z % FULL_Z // HALF, z % HALF
        values = [base_ref[f, level] for f in (0, 1, 2, 3, 7, 4, 5, 6)]
        values[2] = values[2] + float(z - level)
        values[3] = (thole_factor**0.5) * lax.rsqrt(values[3])
        values += [u1_ref[c, level] for c in range(3)]
        values += [u2_ref[c, level] for c in range(3)]
        values += [u3[c, CUTOFF + level] for c in range(3)]
        for n, value in enumerate(values):
            stage[CUTOFF + z, 4 * n : 4 * n + 4] = value[4 * half : 4 * half + 4]

    def staged(z, b):
        return stage[layer * DEPTH + z, pl.ds(b, ROWS, stride=4), :]

    for x in range(SPAN_X):
        begin = (x + HALO - CUTOFF) * WIDE + HALO - CUTOFF
        b, offset = begin // 128, begin % 128
        plane = jnp.where(row < 3, 1.0e3, 0.0)
        for z in range(SPAN_Z):
            goal = z * SPAN_Y
            shift = (goal - offset) % 128
            piece = pltpu.roll(staged(z, b), shift, 1) if shift else staged(z, b)
            if offset + SPAN_Y > 128:
                more = pltpu.roll(staged(z, b + 1), shift, 1) if shift else staged(z, b + 1)
                piece = jnp.where(lane < goal + 128 - offset, piece, more)
            plane = jnp.where((lane >= goal) & (lane < goal + SPAN_Y), piece, plane)
        far_ref[x] = jnp.where(row < FIELDS, plane, 0.0)


def second_kernel(
    layer_ref, base_ref, c3_ref, c5_ref, u1_ref, u2_ref, moment_in, far_ref, moment_ref,
    fields, far, own_sum, partner, partner_sum, vec, vec_b, spots_far, stage,
):
    for f in range(3):
        wrap_levels(lambda level: base_ref[f, level], fields, f, 1.0 if f == 2 else 0.0)
        wrap_levels(lambda level: u2_ref[f, level], vec, f)
    polar_of = lambda level: base_ref[3, level]
    inverse_of = lambda level: 1.0 / base_ref[3, level]
    for number, (dx, dy, _, _) in enumerate(COLUMNS):
        for c in range(3):
            shifted(fields, c, dx * WIDE + dy, spots_far.at[number], c)
    apply_pass(vec, fields, spots_far, c3_ref, c5_ref, far, own_sum, partner, partner_sum)
    finish(polar_of, own_sum, partner_sum, vec_b)
    lay_planes(layer_ref[0], base_ref, u1_ref, u2_ref, vec_b, stage, far_ref)
    lane = lax.broadcasted_iota(jnp.int32, (1, 128), 1)
    moment_ref[...] = jnp.where(lane == 5, inner(vec, vec_b, inverse_of), moment_in[...])


def gradient_kernel(moment_ref, far_ref, dipole_ref, force_ref, energy_ref, turned, out_ref):
    total = jnp.sum(moment_ref[...], axis=0, keepdims=True)
    lane = lax.broadcasted_iota(jnp.int32, (1, 128), 1)

    def pick(n):
        return jnp.sum(jnp.where(lane == n, total, 0.0), axis=1, keepdims=True)

    m0, m1, m2, m3, m4, m5 = (pick(n) for n in range(6))
    g = m2 / (m2 - m3)
    rest = 1.0 - g
    rz1 = rest * rest * m2 + 2.0 * g * rest * m3 + g * g * m4
    a = rest + rz1 / m2
    curve = a * a * (m2 - m3) + 2.0 * a * g * (m3 - m4) + g * g * (m4 - m5)
    g1 = rz1 / curve
    k1 = g + g1 * a
    k2 = g1 * g
    energy_ref[...] = -(m0 + k1 * m1 + k2 * m2)
    far_k1 = jnp.broadcast_to(k1, (1, 128))
    far_k2 = jnp.broadcast_to(k2, (1, 128))

    def plane(x, carry):
        far = []
        for n in range(2 * CUTOFF + 1):
            block = far_ref[x + n]
            spot = [block[c : c + 1] for c in range(5)]
            u = [[block[5 + 3 * q + c : 6 + 3 * q + c] for c in range(3)] for q in range(4)]
            dip = [u[0][c] + far_k1 * u[1][c] + far_k2 * u[2][c] for c in range(3)]
            adj = [u[0][c] + u[1][c] + far_k1 * u[2][c] + far_k2 * u[3][c] for c in range(3)]
            far.append((spot, dip, adj))
        turned[...] = jnp.transpose(far_ref[x + CUTOFF])
        for t in range(DEPTH):
            start = pl.multiple_of(x * (LY * DEPTH) + 8 * t, 8)
            own_block = turned[pl.ds((t + CUTOFF) * SPAN_Y + CUTOFF, LY), :]

            def own_field(n):
                return jnp.broadcast_to(own_block[:, n : n + 1], (8, 128))

            spot_i = [own_field(c) for c in range(5)]
            u = [[own_field(5 + 3 * q + c) for c in range(3)] for q in range(4)]
            dip_i = [u[0][c] + k1 * u[1][c] + k2 * u[2][c] for c in range(3)]
            adj_i = [u[0][c] + u[1][c] + k1 * u[2][c] + k2 * u[3][c] for c in range(3)]
            acc = [jnp.zeros((8, 128), jnp.float32) for _ in range(3)]
            for n in range(2 * CUTOFF + 1):
                spot, dip, adj = far[n]
                d = [spot[c] - spot_i[c] for c in range(3)]
                s = d[0] * d[0] + d[1] * d[1] + d[2] * d[2]
                if n == CUTOFF:
                    own_atom = s == 0.0
                    s = jnp.where(own_atom, 1.0, s)
                inv = lax.rsqrt(s)
                inv2 = inv * inv
                x_damp = (s * s * inv) * (spot_i[3] * spot[3])
                xe = x_damp * jnp.exp(-x_damp)
                e = jnp.exp(-x_damp)
                l3 = 1.0 - e
                l5 = l3 - xe
                cut = jnp.maximum(1.0 - s * (1.0 / (CUTOFF * CUTOFF)), 0.0)
                scale = inv2 * inv
                if n == CUTOFF:
                    scale = jnp.where(spot[4] == spot_i[4], group_scale * scale, scale)
                    scale = jnp.where(own_atom, 0.0, scale)
                ratio = cut * inv2
                scale = scale * cut
                scale5 = 3.0 * scale * inv2
                c5 = scale5 * cut * l5
                slope3 = scale * ((-4.0 / (CUTOFF * CUTOFF)) * l3 - 3.0 * ratio * l5)
                slope5 = scale5 * (
                    (-4.0 / (CUTOFF * CUTOFF)) * l5 + ratio * (3.0 * x_damp * xe - 5.0 * l5)
                )
                own_dip = d[0] * dip_i[0] + d[1] * dip_i[1] + d[2] * dip_i[2]
                own_adj = d[0] * adj_i[0] + d[1] * adj_i[1] + d[2] * adj_i[2]
                far_dip = d[0] * dip[0] + d[1] * dip[1] + d[2] * dip[2]
                far_adj = d[0] * adj[0] + d[1] * adj[1] + d[2] * adj[2]
                cross = (
                    dip_i[0] * adj[0] + dip_i[1] * adj[1] + dip_i[2] * adj[2]
                    + adj_i[0] * dip[0] + adj_i[1] * dip[1] + adj_i[2] * dip[2]
                )
                radial = slope5 * (own_dip * far_adj + own_adj * far_dip) - slope3 * cross
                p1, p2, p3, p4 = c5 * own_dip, c5 * far_adj, c5 * own_adj, c5 * far_dip
                for c in range(3):
                    acc[c] = acc[c] + (
                        radial * d[c] + p1 * adj[c] + p2 * dip_i[c] + p3 * dip[c] + p4 * adj_i[c]
                    )
            lanes = lax.broadcasted_iota(jnp.int32, (8, 128), 1)
            result = jnp.zeros((8, 128), jnp.float32)
            for c in range(3):
                result = jnp.where(lanes == c, dip_i[c], result)
                force = -0.5 * jnp.sum(acc[c], axis=1, keepdims=True)
                result = jnp.where(lanes == 3 + c, force, result)
            out_ref[pl.ds(start, 8), :] = result
        return carry

    lax.fori_loop(0, LX, plane, 0)
    old = lax.broadcasted_iota(jnp.int32, (ATOMS, ATOMS), 0)
    new = lax.broadcasted_iota(jnp.int32, (ATOMS, ATOMS), 1)
    x = new // (LY * DEPTH)
    y = new // DEPTH - LY * x
    z = new - DEPTH * (new // DEPTH)
    order = jnp.where(old == (x * DEPTH + z) * LY + y, 1.0, 0.0)
    result = jnp.dot(
        jnp.transpose(out_ref[...])[:8],
        order,
        precision=lax.Precision.HIGHEST,
        preferred_element_type=jnp.float32,
    )
    for c in range(3):
        dipole_ref[c, 0, 0] = result[c : c + 1]
        force_ref[c, 0, 0] = result[3 + c : 4 + c]


def vmem_specs(count):
    return [pl.BlockSpec(memory_space=pltpu.VMEM)] * count


F32 = jnp.float32
SCRATCH = [
    pltpu.VMEM((5, LEVELS, 8, 128), F32),
    pltpu.VMEM((5, LEVELS, 8, 128), F32),
    pltpu.VMEM((3, HALF, 8, 128), F32),
    pltpu.VMEM((2 * CUTOFF + 1, 3, HALF, 8, 128), F32),
    pltpu.VMEM((3, LEVELS, 8, 128), F32),
    pltpu.VMEM((3, LEVELS, 8, 128), F32),
    pltpu.VMEM((3, LEVELS, 8, 128), F32),
    pltpu.VMEM((len(COLUMNS), 3, LEVELS, 8, 128), F32),
]
COUPLING = jax.ShapeDtypeStruct((OFFSETS, HALF, 8, 128), F32)
VECTOR = jax.ShapeDtypeStruct((3, HALF, 8, 128), F32)
PARAMS = pltpu.CompilerParams(vmem_limit_bytes=16 * 1024 * 1024)


def run_pack(positions, polarizability, direct_field, groups):
    return pl.pallas_call(
        pack_kernel,
        out_shape=jax.ShapeDtypeStruct((LAYERS, 8, ATOMS), F32),
        in_specs=vmem_specs(4),
        out_specs=vmem_specs(1)[0],
        scratch_shapes=[pltpu.VMEM((8, ATOMS), F32)],
        compiler_params=PARAMS,
    )(positions, polarizability, direct_field, groups)


def run_first(base):
    outs = (
        COUPLING,
        COUPLING,
        VECTOR,
        VECTOR,
        jax.ShapeDtypeStruct((1, 128), F32),
    )
    return pl.pallas_call(
        first_kernel,
        out_shape=outs,
        in_specs=vmem_specs(1),
        out_specs=tuple(vmem_specs(len(outs))),
        scratch_shapes=SCRATCH,
        compiler_params=PARAMS,
    )(base)


def run_second(layer, base, c3, c5, u1, u2, moments):
    outs = (
        jax.ShapeDtypeStruct((SPAN_X, ROWS, 128), F32),
        jax.ShapeDtypeStruct((1, 128), F32),
    )
    return pl.pallas_call(
        second_kernel,
        out_shape=outs,
        in_specs=[pl.BlockSpec(memory_space=pltpu.SMEM)] + vmem_specs(6),
        out_specs=tuple(vmem_specs(2)),
        scratch_shapes=SCRATCH + [pltpu.VMEM((FULL_Z + 2 * CUTOFF, 4 * ROWS, 128), F32)],
        compiler_params=PARAMS,
    )(layer, base, c3, c5, u1, u2, moments)


def run_gradient(moments, far):
    return pl.pallas_call(
        gradient_kernel,
        out_shape=(
            jax.ShapeDtypeStruct((3, 1, 1, 1, ATOMS), F32),
            jax.ShapeDtypeStruct((3, 1, 1, 1, ATOMS), F32),
            jax.ShapeDtypeStruct((1, 1), F32),
        ),
        in_specs=vmem_specs(2),
        out_specs=tuple(vmem_specs(3)),
        scratch_shapes=[pltpu.VMEM((128, ROWS), F32), pltpu.VMEM((ATOMS, 128), F32)],
        compiler_params=PARAMS,
    )(moments, far)


def both_sides(low, high, axis):
    count = lax.axis_size(axis)
    below = lax.ppermute(high, axis, [(i, (i + 1) % count) for i in range(count)])
    above = lax.ppermute(low, axis, [((i + 1) % count, i) for i in range(count)])
    return below, above


def widen_x(along_y):
    below, above = both_sides(
        along_y[..., : HALO * WIDE], along_y[..., (LX - HALO) * WIDE :], "gx"
    )
    flat = jnp.concatenate([below, along_y, above], axis=-1)
    flat = jnp.pad(flat, ((0, 0), (0, 0), (0, LANES - WIDE * WIDE)))
    halves = flat.reshape(flat.shape[0], 2, HALF, LANES // 128, 128)
    return halves.transpose(0, 2, 1, 3, 4).reshape(flat.shape[0], HALF, 8, 128)


def join_y(below, own, above):
    lead = own.shape[0]
    return jnp.concatenate([below, own, above], axis=-1).reshape(lead, FULL_Z, LX * WIDE)


def frame_constants():
    place = np.arange(LANES)
    x, y = place // WIDE, place % WIDE
    z = np.arange(FULL_Z)
    full = np.zeros((8, FULL_Z, LANES), np.float32)
    full[0] = (x - HALO)[None, :]
    full[1] = (y - HALO)[None, :]
    full[2] = (z % HALF)[:, None]
    full[3] = np.where(place >= WIDE * WIDE, 0.05, 0.0)[None, :]
    domain = (x + 2) // LX * 8 + (y + 2) // LY
    full[7] = 64.0 * (domain[None, :] * LAYERS + (z // DEPTH)[:, None])
    halves = full.reshape(8, 2, HALF, LANES // 128, 128).transpose(0, 2, 1, 3, 4)
    return halves.reshape(8, HALF, 8, 128)


def on_device(positions, polarizability, direct_field, groups):
    layer = lax.axis_index("gz")
    copies = run_pack(positions, polarizability, direct_field, groups)
    column = lax.all_to_all(copies, "gz", 0, 0)
    below, above = both_sides(column, column, "gy")
    lattices = [
        part.reshape(LAYERS, 8, DEPTH, LX, LY).transpose(1, 0, 2, 3, 4).reshape(8, FULL_Z, LX, LY)
        for part in (below, column, above)
    ]
    along_y = join_y(lattices[0][..., LY - HALO :], lattices[1], lattices[2][..., :HALO])
    base = widen_x(along_y) + frame_constants()
    c3, c5, u1, u2, moments = run_first(base)
    flat_u2 = u2.reshape(3, HALF, 2, LANES).transpose(0, 2, 1, 3).reshape(3, FULL_Z, LANES)
    own_u2 = flat_u2[..., HALO * WIDE : (HALO + LX) * WIDE].reshape(3, FULL_Z, LX, WIDE)
    own_u2 = own_u2[..., HALO : HALO + LY]
    low = own_u2[..., :HALO].reshape(3, FULL_Z, LX * HALO)
    high = own_u2[..., LY - HALO :].reshape(3, FULL_Z, LX * HALO)
    below, above = both_sides(low, high, "gy")
    cut = (3, FULL_Z, LX, HALO)
    u2_wide = widen_x(join_y(below.reshape(cut), own_u2, above.reshape(cut)))
    far, moments = run_second(layer[None], base, c3, c5, u1, u2_wide, moments)
    moments, far = lax.optimization_barrier((moments, far))
    for axis in ("gx", "gy"):
        count = lax.axis_size(axis)
        copies = jnp.broadcast_to(moments[None], (count, 1, 128))
        moments = lax.all_to_all(copies, axis, 0, 0).reshape(count, 128)
        if axis == "gx":
            moments = jnp.sum(moments, axis=0, keepdims=True)
    dipoles, gradient, energy = run_gradient(moments, far)
    devices = lax.axis_size("gx") * lax.axis_size("gy") * lax.axis_size("gz")
    return (dipoles, gradient, (energy / (2.0 * ATOMS * devices)).reshape(()))


def solution(mesh):
    along = ("gx", "gy", "gz", None)
    return jax.shard_map(
        on_device,
        mesh=mesh,
        in_specs=(P(None, *along), P(*along), P(None, *along), P(*along)),
        out_specs=(P(None, *along), P(None, *along), P()),
        check_vma=False,
    )
```

```python
import numpy as np

import jax
import jax.numpy as jnp
from jax import lax
from jax.experimental import pallas as pl
from jax.experimental.pallas import tpu as pltpu
from jax.sharding import PartitionSpec as P

LX = 8
LY = 8
DEPTH = 3
CUTOFF = 3
LAYERS = 4
FULL_Z = DEPTH * LAYERS
HALO = 2 * CUTOFF
WIDE = LX + 2 * HALO
ATOMS = LX * LY * DEPTH
ROWS = 24
LANES = 512
HALF = FULL_Z // 2
LEVELS = HALF + 2 * CUTOFF
JITTER = 0.4
SPAN_X = LX + 2 * CUTOFF
SPAN_Y = LY + 2 * CUTOFF
SPAN_Z = DEPTH + 2 * CUTOFF
FIELDS = 17

thole_factor = 0.39
group_scale = 0.5


def within(dx, dy, dz):
    least = sum(max(abs(o) - JITTER, 0.0) ** 2 for o in (dx, dy, dz))
    return least < CUTOFF * CUTOFF


def half_offsets():
    reach = range(-CUTOFF, CUTOFF + 1)
    columns = []
    count = 0
    for dx in range(0, CUTOFF + 1):
        for dy in reach:
            depths = [
                dz
                for dz in reach
                if (dx > 0 or dy > 0 or (dy == 0 and dz > 0)) and within(dx, dy, dz)
            ]
            if depths:
                columns.append((dx, dy, depths, count))
                count += len(depths)
    return columns, count


COLUMNS, OFFSETS = half_offsets()


def may_share_group(dx, dy, dz):
    return dx == 0 and abs(DEPTH * dy + dz) <= 7 and abs(dz) < DEPTH


def lane_iota(rows=8):
    return lax.broadcasted_iota(jnp.int32, (rows, 128), 1)


def wrap_levels(value_of, out, slot, lift=0.0):
    for level in range(HALF):
        value = value_of(level)
        out[slot, CUTOFF + level] = value
        if level < CUTOFF:
            out[slot, CUTOFF + HALF + level] = pltpu.roll(value, 4, 0) + lift * HALF
        if level >= HALF - CUTOFF:
            out[slot, CUTOFF - HALF + level] = pltpu.roll(value, 4, 0) - lift * HALF


def shifted(source, field, shift, out, slot):
    if shift == 0:
        for level in range(LEVELS):
            out[slot, level] = source[field, level]
        return
    keep = lane_iota() >= shift
    for level in range(LEVELS):
        here = source[field, level]
        both = jnp.where(keep, here, pltpu.roll(here, 7, 0))
        out[slot, level] = pltpu.roll(both, 128 - shift, 1)


def spread(values, depths, shift, total):
    keep = lane_iota() >= shift
    for c in range(3):
        for level in range(-CUTOFF, HALF + CUTOFF):
            shares = [
                values[n, c, level - dz] for n, dz in enumerate(depths) if 0 <= level - dz < HALF
            ]
            if not shares:
                continue
            while len(shares) > 1:
                shares = [sum(shares[i : i + 2]) for i in range(0, len(shares), 2)]
            part = shares[0]
            if shift:
                turned = pltpu.roll(part, shift, 1)
                part = jnp.where(keep, turned, pltpu.roll(turned, 1, 0))
            total[c, CUTOFF + level] += part


def finish(polar_of, own_sum, partner_sum, out):
    for c in range(3):

        def value_of(level):
            other = CUTOFF + level + (HALF if level < CUTOFF else -HALF)
            folded = own_sum[c, level] + partner_sum[c, CUTOFF + level]
            return (folded + pltpu.roll(partner_sum[c, other], 4, 0)) * polar_of(level)

        wrap_levels(value_of, out, c)


def own_places():
    block = lax.broadcasted_iota(jnp.int32, (8, 128), 0)
    place = lane_iota() + 128 * jnp.where(block >= 4, block - 4, block)
    x = place // WIDE
    y = place - x * WIDE
    return (x >= HALO) & (x < HALO + LX) & (y >= HALO) & (y < HALO + LY)


def inner(first, second, inverse_of):
    total = jnp.zeros((8, 128), jnp.float32)
    for level in range(HALF):
        at = CUTOFF + level
        total = total + sum(first[c, at] * second[c, at] for c in range(3)) * inverse_of(level)
    return jnp.sum(jnp.where(own_places(), total, 0.0))


def apply_pass(vec, spots, spots_far, c3_ref, c5_ref, far, own_sum, partner, partner_sum):
    own_sum[...] = jnp.zeros_like(own_sum)
    partner_sum[...] = jnp.zeros_like(partner_sum)
    for number, (dx, dy, depths, first) in enumerate(COLUMNS):
        shift = dx * WIDE + dy
        for c in range(3):
            shifted(vec, c, shift, far, c)

        def per_level(level, carry):
            own = [spots[c, CUTOFF + level] for c in range(3)]
            own_u = [vec[c, CUTOFF + level] for c in range(3)]
            acc = [own_sum[c, level] for c in range(3)]
            for n, dz in enumerate(depths):
                at = CUTOFF + dz + level
                d = [spots_far[number, c, at] - own[c] for c in range(3)]
                far_u = [far[c, at] for c in range(3)]
                c3 = c3_ref[first + n, level]
                c5 = c5_ref[first + n, level]
                along_far = c5 * (d[0] * far_u[0] + d[1] * far_u[1] + d[2] * far_u[2])
                along_own = c5 * (d[0] * own_u[0] + d[1] * own_u[1] + d[2] * own_u[2])
                for c in range(3):
                    acc[c] = acc[c] + (along_far * d[c] - c3 * far_u[c])
                    partner[n, c, level] = along_own * d[c] - c3 * own_u[c]
            for c in range(3):
                own_sum[c, level] = acc[c]
            return carry

        lax.fori_loop(0, HALF, per_level, 0, unroll=6)
        spread(partner, depths, shift, partner_sum)


def pack_kernel(input_ref, out_ref, rows):
    site = lax.broadcasted_iota(jnp.int32, (1, ATOMS), 1)
    x = site // (LY * DEPTH)
    y = site // DEPTH - LY * x
    z = site - DEPTH * (site // DEPTH)
    for c, lattice in enumerate((x, y, z)):
        rows[c : c + 1] = input_ref[c, 0, 0] - lattice.astype(jnp.float32)
        rows[4 + c : 5 + c] = input_ref[3, 0, 0] * input_ref[4 + c, 0, 0]
    rows[3:4] = input_ref[3, 0, 0]
    rows[7:8] = input_ref[7, 0, 0]
    old = lax.broadcasted_iota(jnp.int32, (ATOMS, ATOMS), 0)
    new = lax.broadcasted_iota(jnp.int32, (ATOMS, ATOMS), 1)
    plane = new // (LX * LY)
    order = jnp.where(old == DEPTH * (new - LX * LY * plane) + plane, 1.0, 0.0)
    packed = jnp.dot(
        rows[...], order, precision=lax.Precision.HIGHEST, preferred_element_type=jnp.float32
    )
    for n in range(LAYERS):
        out_ref[n] = packed


def first_kernel(
    base_ref, c3_ref, c5_ref, u1_ref, u2_ref, moment_ref,
    fields, far, own_sum, partner, partner_sum, vec, vec_b, spots_far,
):
    for f in range(3):
        wrap_levels(lambda level: base_ref[f, level], fields, f, 1.0 if f == 2 else 0.0)
        wrap_levels(lambda level: base_ref[4 + f, level], vec, f)
    wrap_levels(lambda level: (thole_factor**0.5) * lax.rsqrt(base_ref[3, level]), fields, 3)
    wrap_levels(lambda level: base_ref[7, level], fields, 4)
    polar_of = lambda level: base_ref[3, level]
    inverse_of = lambda level: 1.0 / base_ref[3, level]

    own_sum[...] = jnp.zeros_like(own_sum)
    partner_sum[...] = jnp.zeros_like(partner_sum)
    for number, (dx, dy, depths, first) in enumerate(COLUMNS):
        shift = dx * WIDE + dy
        for c in range(3):
            shifted(fields, c, shift, spots_far.at[number], c)
            shifted(vec, c, shift, far, c)
        shifted(fields, 3, shift, far, 3)
        if dx == 0:
            shifted(fields, 4, shift, far, 4)

        def per_level(level, carry):
            own = [fields[c, CUTOFF + level] for c in range(3)]
            root = fields[3, CUTOFF + level]
            own_u = [vec[c, CUTOFF + level] for c in range(3)]
            acc = [own_sum[c, level] for c in range(3)]
            for n, dz in enumerate(depths):
                at = CUTOFF + dz + level
                d = [spots_far[number, c, at] - own[c] for c in range(3)]
                far_u = [far[c, at] for c in range(3)]
                s = d[0] * d[0] + d[1] * d[1] + d[2] * d[2]
                inv = lax.rsqrt(s)
                inv2 = inv * inv
                inv3 = inv2 * inv
                x = (s * s * inv) * (root * far[3, at])
                e = jnp.exp(-x)
                l3 = 1.0 - e
                l5 = l3 - x * e
                cut = jnp.maximum(1.0 - s * (1.0 / (CUTOFF * CUTOFF)), 0.0)
                weight = cut * cut * inv3
                if may_share_group(dx, dy, dz):
                    same = fields[4, CUTOFF + level] == far[4, at]
                    weight = jnp.where(same, group_scale * weight, weight)
                c3 = weight * l3
                c5 = (3.0 * weight) * (inv2 * l5)
                c3_ref[first + n, level] = c3
                c5_ref[first + n, level] = c5
                along_far = c5 * (d[0] * far_u[0] + d[1] * far_u[1] + d[2] * far_u[2])
                along_own = c5 * (d[0] * own_u[0] + d[1] * own_u[1] + d[2] * own_u[2])
                for c in range(3):
                    acc[c] = acc[c] + (along_far * d[c] - c3 * far_u[c])
                    partner[n, c, level] = along_own * d[c] - c3 * own_u[c]
            for c in range(3):
                own_sum[c, level] = acc[c]
            return carry

        lax.fori_loop(0, HALF, per_level, 0, unroll=6)
        spread(partner, depths, shift, partner_sum)
    finish(polar_of, own_sum, partner_sum, vec_b)
    moments = [inner(vec, vec, inverse_of), inner(vec, vec_b, inverse_of), inner(vec_b, vec_b, inverse_of)]
    for c in range(3):
        for level in range(HALF):
            u1_ref[c, level] = vec_b[c, CUTOFF + level]
    apply_pass(vec_b, fields, spots_far, c3_ref, c5_ref, far, own_sum, partner, partner_sum)
    finish(polar_of, own_sum, partner_sum, vec)
    moments += [inner(vec_b, vec, inverse_of), inner(vec, vec, inverse_of)]
    for c in range(3):
        for level in range(HALF):
            u2_ref[c, level] = vec[c, CUTOFF + level]
    lane = lax.broadcasted_iota(jnp.int32, (1, 128), 1)
    row = jnp.zeros((1, 128), jnp.float32)
    for n, value in enumerate(moments):
        row = jnp.where(lane == n, value, row)
    moment_ref[...] = row


def lay_planes(layer, base_ref, u1_ref, u2_ref, u3, stage, far_ref):
    lane = lane_iota(ROWS)
    row = lax.broadcasted_iota(jnp.int32, (ROWS, 128), 0)
    for z in range(-CUTOFF, FULL_Z + CUTOFF):
        half, level = z % FULL_Z // HALF, z % HALF
        values = [base_ref[f, level] for f in (0, 1, 2, 3, 7, 4, 5, 6)]
        values[2] = values[2] + float(z - level)
        values[3] = (thole_factor**0.5) * lax.rsqrt(values[3])
        values += [u1_ref[c, level] for c in range(3)]
        values += [u2_ref[c, level] for c in range(3)]
        values += [u3[c, CUTOFF + level] for c in range(3)]
        for n, value in enumerate(values):
            stage[CUTOFF + z, 4 * n : 4 * n + 4] = value[4 * half : 4 * half + 4]

    def staged(z, b):
        return stage[layer * DEPTH + z, pl.ds(b, ROWS, stride=4), :]

    for x in range(SPAN_X):
        begin = (x + HALO - CUTOFF) * WIDE + HALO - CUTOFF
        b, offset = begin // 128, begin % 128
        plane = jnp.where(row < 3, 1.0e3, 0.0)
        for z in range(SPAN_Z):
            goal = z * SPAN_Y
            shift = (goal - offset) % 128
            piece = pltpu.roll(staged(z, b), shift, 1) if shift else staged(z, b)
            if offset + SPAN_Y > 128:
                more = pltpu.roll(staged(z, b + 1), shift, 1) if shift else staged(z, b + 1)
                piece = jnp.where(lane < goal + 128 - offset, piece, more)
            plane = jnp.where((lane >= goal) & (lane < goal + SPAN_Y), piece, plane)
        far_ref[x] = jnp.where(row < FIELDS, plane, 0.0)


def second_kernel(
    layer_ref, base_ref, c3_ref, c5_ref, u1_ref, u2_ref, moment_in, far_ref, moment_ref,
    fields, far, own_sum, partner, partner_sum, vec, vec_b, spots_far, stage,
):
    for f in range(3):
        wrap_levels(lambda level: base_ref[f, level], fields, f, 1.0 if f == 2 else 0.0)
        wrap_levels(lambda level: u2_ref[f, level], vec, f)
    polar_of = lambda level: base_ref[3, level]
    inverse_of = lambda level: 1.0 / base_ref[3, level]
    for number, (dx, dy, _, _) in enumerate(COLUMNS):
        for c in range(3):
            shifted(fields, c, dx * WIDE + dy, spots_far.at[number], c)
    apply_pass(vec, fields, spots_far, c3_ref, c5_ref, far, own_sum, partner, partner_sum)
    finish(polar_of, own_sum, partner_sum, vec_b)
    lay_planes(layer_ref[0], base_ref, u1_ref, u2_ref, vec_b, stage, far_ref)
    lane = lax.broadcasted_iota(jnp.int32, (1, 128), 1)
    moment_ref[...] = jnp.where(lane == 5, inner(vec, vec_b, inverse_of), moment_in[...])


def gradient_kernel(
    moment_ref, far_ref, dipole_ref, force_ref, energy_ref, turned, out_ref, wide
):
    total = jnp.sum(moment_ref[...], axis=0, keepdims=True)
    lane = lax.broadcasted_iota(jnp.int32, (1, 128), 1)

    def pick(n):
        return jnp.sum(jnp.where(lane == n, total, 0.0), axis=1, keepdims=True)

    m0, m1, m2, m3, m4, m5 = (pick(n) for n in range(6))
    g = m2 / (m2 - m3)
    rest = 1.0 - g
    rz1 = rest * rest * m2 + 2.0 * g * rest * m3 + g * g * m4
    a = rest + rz1 / m2
    curve = a * a * (m2 - m3) + 2.0 * a * g * (m3 - m4) + g * g * (m4 - m5)
    g1 = rz1 / curve
    k1 = g + g1 * a
    k2 = g1 * g
    energy_ref[...] = -(m0 + k1 * m1 + k2 * m2)
    far_k1 = jnp.broadcast_to(k1, (1, 128))
    far_k2 = jnp.broadcast_to(k2, (1, 128))

    for x in range(SPAN_X):
        block = far_ref[x]
        u = [[block[5 + 3 * q + c : 6 + 3 * q + c] for c in range(3)] for q in range(4)]
        values = [block[c : c + 1] for c in range(5)]
        values += [u[0][c] + far_k1 * u[1][c] + far_k2 * u[2][c] for c in range(3)]
        values += [u[0][c] + u[1][c] + far_k1 * u[2][c] + far_k2 * u[3][c] for c in range(3)]
        for n, value in enumerate(values):
            wide[x, n] = jnp.broadcast_to(value, (8, 128))

    def plane(x, carry):
        turned[x] = jnp.transpose(far_ref[x + CUTOFF])
        for t in range(DEPTH):
            start = pl.multiple_of(x * (LY * DEPTH) + 8 * t, 8)
            own_block = turned[x, pl.ds((t + CUTOFF) * SPAN_Y + CUTOFF, LY), :]

            def own_field(n):
                return jnp.broadcast_to(own_block[:, n : n + 1], (8, 128))

            spot_i = [own_field(c) for c in range(5)]
            u = [[own_field(5 + 3 * q + c) for c in range(3)] for q in range(4)]
            dip_i = [u[0][c] + k1 * u[1][c] + k2 * u[2][c] for c in range(3)]
            adj_i = [u[0][c] + u[1][c] + k1 * u[2][c] + k2 * u[3][c] for c in range(3)]
            acc = [jnp.zeros((8, 128), jnp.float32) for _ in range(3)]
            for n in range(2 * CUTOFF + 1):
                spot = [wide[x + n, c] for c in range(5 if n == CUTOFF else 4)]
                dip = [wide[x + n, 5 + c] for c in range(3)]
                adj = [wide[x + n, 8 + c] for c in range(3)]
                d = [spot[c] - spot_i[c] for c in range(3)]
                s = d[0] * d[0] + d[1] * d[1] + d[2] * d[2]
                if n == CUTOFF:
                    own_atom = s == 0.0
                    s = jnp.where(own_atom, 1.0, s)
                inv = lax.rsqrt(s)
                inv2 = inv * inv
                x_damp = (s * s * inv) * (spot_i[3] * spot[3])
                e = jnp.exp(-x_damp)
                xe = x_damp * e
                l3 = 1.0 - e
                l5 = l3 - xe
                cut = jnp.maximum(1.0 - s * (1.0 / (CUTOFF * CUTOFF)), 0.0)
                scale = inv2 * inv
                if n == CUTOFF:
                    scale = jnp.where(spot[4] == spot_i[4], group_scale * scale, scale)
                    scale = jnp.where(own_atom, 0.0, scale)
                ratio = cut * inv2
                scale = scale * cut
                scale5 = 3.0 * scale * inv2
                c5 = scale5 * cut * l5
                slope3 = scale * ((-4.0 / (CUTOFF * CUTOFF)) * l3 - 3.0 * ratio * l5)
                slope5 = scale5 * (
                    (-4.0 / (CUTOFF * CUTOFF)) * l5 + ratio * (3.0 * x_damp * xe - 5.0 * l5)
                )
                own_dip = d[0] * dip_i[0] + d[1] * dip_i[1] + d[2] * dip_i[2]
                own_adj = d[0] * adj_i[0] + d[1] * adj_i[1] + d[2] * adj_i[2]
                far_dip = d[0] * dip[0] + d[1] * dip[1] + d[2] * dip[2]
                far_adj = d[0] * adj[0] + d[1] * adj[1] + d[2] * adj[2]
                cross = (
                    dip_i[0] * adj[0] + dip_i[1] * adj[1] + dip_i[2] * adj[2]
                    + adj_i[0] * dip[0] + adj_i[1] * dip[1] + adj_i[2] * dip[2]
                )
                radial = slope5 * (own_dip * far_adj + own_adj * far_dip) - slope3 * cross
                p1, p2, p3, p4 = c5 * own_dip, c5 * far_adj, c5 * own_adj, c5 * far_dip
                for c in range(3):
                    acc[c] = acc[c] + (
                        radial * d[c] + p1 * adj[c] + p2 * dip_i[c] + p3 * dip[c] + p4 * adj_i[c]
                    )
            lanes = lax.broadcasted_iota(jnp.int32, (8, 128), 1)
            result = jnp.zeros((8, 128), jnp.float32)
            for c in range(3):
                result = jnp.where(lanes == c, dip_i[c], result)
                force = -0.5 * jnp.sum(acc[c], axis=1, keepdims=True)
                result = jnp.where(lanes == 3 + c, force, result)
            out_ref[pl.ds(start, 8), :] = result
        return carry

    lax.fori_loop(0, LX, plane, 0, unroll=2)
    old = lax.broadcasted_iota(jnp.int32, (ATOMS, ATOMS), 0)
    new = lax.broadcasted_iota(jnp.int32, (ATOMS, ATOMS), 1)
    x = new // (LY * DEPTH)
    y = new // DEPTH - LY * x
    z = new - DEPTH * (new // DEPTH)
    order = jnp.where(old == (x * DEPTH + z) * LY + y, 1.0, 0.0)
    result = jnp.dot(
        jnp.transpose(out_ref[...])[:8],
        order,
        precision=lax.Precision.HIGHEST,
        preferred_element_type=jnp.float32,
    )
    for c in range(3):
        dipole_ref[c, 0, 0] = result[c : c + 1]
        force_ref[c, 0, 0] = result[3 + c : 4 + c]


def vmem_specs(count):
    return [pl.BlockSpec(memory_space=pltpu.VMEM)] * count


F32 = jnp.float32
SCRATCH = [
    pltpu.VMEM((5, LEVELS, 8, 128), F32),
    pltpu.VMEM((5, LEVELS, 8, 128), F32),
    pltpu.VMEM((3, HALF, 8, 128), F32),
    pltpu.VMEM((2 * CUTOFF + 1, 3, HALF, 8, 128), F32),
    pltpu.VMEM((3, LEVELS, 8, 128), F32),
    pltpu.VMEM((3, LEVELS, 8, 128), F32),
    pltpu.VMEM((3, LEVELS, 8, 128), F32),
    pltpu.VMEM((len(COLUMNS), 3, LEVELS, 8, 128), F32),
]
COUPLING = jax.ShapeDtypeStruct((OFFSETS, HALF, 8, 128), F32)
VECTOR = jax.ShapeDtypeStruct((3, HALF, 8, 128), F32)
PARAMS = pltpu.CompilerParams(vmem_limit_bytes=16 * 1024 * 1024)


def run_pack(positions, polarizability, direct_field, groups):
    return pl.pallas_call(
        pack_kernel,
        out_shape=jax.ShapeDtypeStruct((LAYERS, 8, ATOMS), F32),
        in_specs=vmem_specs(1),
        out_specs=vmem_specs(1)[0],
        scratch_shapes=[pltpu.VMEM((8, ATOMS), F32)],
        compiler_params=PARAMS,
    )(jnp.concatenate([positions, polarizability[None], direct_field, groups[None].astype(F32)]))


def run_first(base):
    outs = (
        COUPLING,
        COUPLING,
        VECTOR,
        VECTOR,
        jax.ShapeDtypeStruct((1, 128), F32),
    )
    return pl.pallas_call(
        first_kernel,
        out_shape=outs,
        in_specs=vmem_specs(1),
        out_specs=tuple(vmem_specs(len(outs))),
        scratch_shapes=SCRATCH,
        compiler_params=PARAMS,
    )(base)


def run_second(layer, base, c3, c5, u1, u2, moments):
    outs = (
        jax.ShapeDtypeStruct((SPAN_X, ROWS, 128), F32),
        jax.ShapeDtypeStruct((1, 128), F32),
    )
    return pl.pallas_call(
        second_kernel,
        out_shape=outs,
        in_specs=[pl.BlockSpec(memory_space=pltpu.SMEM)] + vmem_specs(6),
        out_specs=tuple(vmem_specs(2)),
        scratch_shapes=SCRATCH + [pltpu.VMEM((FULL_Z + 2 * CUTOFF, 4 * ROWS, 128), F32)],
        compiler_params=PARAMS,
    )(layer, base, c3, c5, u1, u2, moments)


def run_gradient(moments, far):
    return pl.pallas_call(
        gradient_kernel,
        out_shape=(
            jax.ShapeDtypeStruct((3, 1, 1, 1, ATOMS), F32),
            jax.ShapeDtypeStruct((3, 1, 1, 1, ATOMS), F32),
            jax.ShapeDtypeStruct((1, 1), F32),
        ),
        in_specs=vmem_specs(2),
        out_specs=tuple(vmem_specs(3)),
        scratch_shapes=[
            pltpu.VMEM((LX, 128, ROWS), F32),
            pltpu.VMEM((ATOMS, 128), F32),
            pltpu.VMEM((SPAN_X, 11, 8, 128), F32),
        ],
        compiler_params=PARAMS,
    )(moments, far)


def both_sides(low, high, axis):
    count = lax.axis_size(axis)
    below = lax.ppermute(high, axis, [(i, (i + 1) % count) for i in range(count)])
    above = lax.ppermute(low, axis, [((i + 1) % count, i) for i in range(count)])
    return below, above


def widen_x(along_y):
    below, above = both_sides(
        along_y[..., : HALO * WIDE], along_y[..., (LX - HALO) * WIDE :], "gx"
    )
    flat = jnp.concatenate([below, along_y, above], axis=-1)
    flat = jnp.pad(flat, ((0, 0), (0, 0), (0, LANES - WIDE * WIDE)))
    halves = flat.reshape(flat.shape[0], 2, HALF, LANES // 128, 128)
    return halves.transpose(0, 2, 1, 3, 4).reshape(flat.shape[0], HALF, 8, 128)


def join_y(below, own, above):
    lead = own.shape[0]
    return jnp.concatenate([below, own, above], axis=-1).reshape(lead, FULL_Z, LX * WIDE)


def frame_constants():
    place = np.arange(LANES)
    x, y = place // WIDE, place % WIDE
    z = np.arange(FULL_Z)
    full = np.zeros((8, FULL_Z, LANES), np.float32)
    full[0] = (x - HALO)[None, :]
    full[1] = (y - HALO)[None, :]
    full[2] = (z % HALF)[:, None]
    full[3] = np.where(place >= WIDE * WIDE, 0.05, 0.0)[None, :]
    domain = (x + 2) // LX * 8 + (y + 2) // LY
    full[7] = 64.0 * (domain[None, :] * LAYERS + (z // DEPTH)[:, None])
    halves = full.reshape(8, 2, HALF, LANES // 128, 128).transpose(0, 2, 1, 3, 4)
    return halves.reshape(8, HALF, 8, 128)


def on_device(positions, polarizability, direct_field, groups):
    layer = lax.axis_index("gz")
    copies = run_pack(positions, polarizability, direct_field, groups)
    column = lax.all_to_all(copies, "gz", 0, 0)
    below, above = both_sides(column, column, "gy")
    lattices = [
        part.reshape(LAYERS, 8, DEPTH, LX, LY).transpose(1, 0, 2, 3, 4).reshape(8, FULL_Z, LX, LY)
        for part in (below, column, above)
    ]
    along_y = join_y(lattices[0][..., LY - HALO :], lattices[1], lattices[2][..., :HALO])
    base = widen_x(along_y) + frame_constants()
    c3, c5, u1, u2, moments = run_first(base)
    flat_u2 = u2.reshape(3, HALF, 2, LANES).transpose(0, 2, 1, 3).reshape(3, FULL_Z, LANES)
    own_u2 = flat_u2[..., HALO * WIDE : (HALO + LX) * WIDE].reshape(3, FULL_Z, LX, WIDE)
    own_u2 = own_u2[..., HALO : HALO + LY]
    low = own_u2[..., :HALO].reshape(3, FULL_Z, LX * HALO)
    high = own_u2[..., LY - HALO :].reshape(3, FULL_Z, LX * HALO)
    below, above = both_sides(low, high, "gy")
    cut = (3, FULL_Z, LX, HALO)
    u2_wide = widen_x(join_y(below.reshape(cut), own_u2, above.reshape(cut)))
    far, moments = run_second(layer[None], base, c3, c5, u1, u2_wide, moments)
    moments, far = lax.optimization_barrier((moments, far))
    for axis in ("gx", "gy"):
        count = lax.axis_size(axis)
        copies = jnp.broadcast_to(moments[None], (count, 1, 128))
        moments = lax.all_to_all(copies, axis, 0, 0).reshape(count, 128)
        if axis == "gx":
            moments = jnp.sum(moments, axis=0, keepdims=True)
    dipoles, gradient, energy = run_gradient(moments, far)
    devices = lax.axis_size("gx") * lax.axis_size("gy") * lax.axis_size("gz")
    return (dipoles, gradient, (energy / (2.0 * ATOMS * devices)).reshape(()))


def solution(mesh):
    along = ("gx", "gy", "gz", None)
    return jax.shard_map(
        on_device,
        mesh=mesh,
        in_specs=(P(None, *along), P(*along), P(None, *along), P(*along)),
        out_specs=(P(None, *along), P(None, *along), P()),
        check_vma=False,
    )
```
